512 devices in a mesh: aa: 32 (over y_lo, z, core), ba: 16 (over x, y_hi).
Axes of the slice: x: 4, y: 8 (y_hi: 4, y_lo: 2; y = y_hi * 2 + y_lo), z: 8, core: 2. Of those that a mesh axis runs over, the one named last changes fastest.
Arguments:
- frame_one: bfloat16 [32768, 128], P('aa'), may hold values from -40 to 40
- frame_two: bfloat16 [32768, 128], P('ba'), may hold values from -40 to 40
Outputs:
- warped_one: float32 [32768, 128], P(('aa', 'ba'))
- flow_one: float32 [2, 32768], P(None, ('aa', 'ba'))
- warped_two: float32 [32768, 128], P(('ba', 'aa'))
- flow_two: float32 [2, 32768], P(None, ('ba', 'aa'))
The draws below stay inside these ranges and needn't reach their ends.
All inputs are finite; a program needn't handle non-finite values.
Results may differ from the reference program's by a relative error of at most 0.0039.
Values sent between devices are 32-bit elements; how exact they have to be, the bound alone decides.
A program may use at most 64 MiB of HBM per device.

```python
import jax
import jax.numpy as jnp
from jax import lax

CHANNELS = 128
IMG_W = 128
PIXELS = 32768


def shared_parts(key):
    base = jnp.clip(jax.random.normal(jax.random.fold_in(key, 11), (PIXELS, CHANNELS), jnp.float32), -6.0, 6.0)
    noise = jnp.clip(jax.random.normal(jax.random.fold_in(key, 12), (PIXELS, CHANNELS), jnp.float32), -6.0, 6.0)
    source = jax.random.randint(jax.random.fold_in(key, 13), (PIXELS,), 0, PIXELS)
    position = jnp.arange(PIXELS, dtype=jnp.int32)
    source = jnp.where(position % 613 < 2, position // 613 * 613, source)
    return (base, noise, source)


def draw_frame_one(key, part):
    base, noise, source = shared_parts(key)
    values = 1.1 * base
    return values.astype(jnp.bfloat16)


def draw_frame_two(key, part):
    base, noise, source = shared_parts(key)
    matched = base[source]
    values = 1.1 * (0.76 * matched + 0.65 * noise)
    return values.astype(jnp.bfloat16)


def setup_inputs(seed: int = 0) -> dict:
    arg_keys = jax.random.split(jax.random.key(seed), 3)
    frame_one = draw_frame_one(jax.random.fold_in(arg_keys[2], 71), 0)
    frame_two = draw_frame_two(jax.random.fold_in(arg_keys[2], 71), 0)
    return dict(frame_one=frame_one, frame_two=frame_two)


def pixel_grid(start_pos, total_rows):
    position = start_pos + jnp.arange(total_rows, dtype=jnp.int32)
    column_pos = (position % IMG_W).astype(jnp.float32) / 64.0
    row_pos = (position // IMG_W).astype(jnp.float32) / 64.0
    return jnp.stack([column_pos, row_pos]).astype(jnp.bfloat16)


def reference(frame_one, frame_two):
    factor = CHANNELS ** -0.5
    grid_one = pixel_grid(0, PIXELS)
    grid_two = grid_one
    block_rows = 256 if PIXELS % 256 == 0 else PIXELS
    block_count = PIXELS // block_rows
    tiles = frame_one.reshape(block_count, block_rows, CHANNELS)
    grid_tiles = grid_one.reshape(2, block_count, block_rows).transpose(1, 0, 2)

    def scores(tile_rows):
        return lax.dot_general(tile_rows, frame_two, (((1,), (1,)), ((), ())), preferred_element_type=jnp.float32) * factor

    def first_pass(state_pair, tile_rows):
        scores_now = scores(tile_rows)
        row_peak = scores_now.max(axis=1)
        row_total = jnp.exp(scores_now - row_peak[:, None]).sum(axis=1)
        col_peak = jnp.maximum(state_pair[0], scores_now.max(axis=0))
        col_total = state_pair[1] * jnp.exp(state_pair[0] - col_peak) + jnp.exp(scores_now - col_peak[None, :]).sum(axis=0)
        return (col_peak, col_total), (row_peak, row_total)

    start_state = (jnp.full((PIXELS,), -jnp.inf, jnp.float32), jnp.zeros((PIXELS,), jnp.float32))
    (col_peak, col_total), (row_peaks, row_totals) = lax.scan(first_pass, start_state, tiles)

    def second_pass(state_pair, inputs):
        tile_rows, tile_grid, row_peak, row_total = inputs
        scores_now = scores(tile_rows)
        forward = (jnp.exp(scores_now - row_peak[:, None]) / row_total[:, None]).astype(jnp.bfloat16)
        backward = (jnp.exp(scores_now - col_peak[None, :]) / col_total[None, :]).astype(jnp.bfloat16)
        forward_feat = jnp.dot(forward, frame_two, preferred_element_type=jnp.float32)
        forward_coord = lax.dot_general(grid_two, forward, (((1,), (1,)), ((), ())), preferred_element_type=jnp.float32)
        back_feat = state_pair[0] + lax.dot_general(backward, tile_rows, (((0,), (0,)), ((), ())), preferred_element_type=jnp.float32)
        back_coord = state_pair[1] + jnp.dot(tile_grid, backward, preferred_element_type=jnp.float32)
        return (back_feat, back_coord), (forward_feat, forward_coord)

    start_back = (jnp.zeros((PIXELS, CHANNELS), jnp.float32), jnp.zeros((2, PIXELS), jnp.float32))
    (back_feat, back_coord), (forward_feat, forward_coord) = lax.scan(
        second_pass, start_back, (tiles, grid_tiles, row_peaks, row_totals))
    warped_one = forward_feat.reshape(PIXELS, CHANNELS)
    flow_one = forward_coord.transpose(1, 0, 2).reshape(2, PIXELS) - grid_one.astype(jnp.float32)
    warped_two = back_feat
    flow_two = back_coord - grid_two.astype(jnp.float32)
    return (warped_one, flow_one, warped_two, flow_two)
```

```python
import functools
import math

import jax
import jax.numpy as jnp
from jax import lax
from jax.experimental import pallas as pl
from jax.experimental.pallas import tpu as pltpu
from jax.sharding import PartitionSpec as P

IMG_W = 128
CH = 128
MSG = CH + 8
AUG = CH + 16
CHUNK = 256
PART = 64
PACK = PART + 8
SCALE = CH ** (-0.5) * math.log2(math.e)
MESH = pl.DeviceIdType.MESH
F32 = jnp.float32
BF16 = jnp.bfloat16


def grid_xy(pixel):
    column_pos = lax.rem(pixel, IMG_W).astype(F32) / 64.0
    row_pos = lax.div(pixel, IMG_W).astype(F32) / 64.0
    return column_pos, row_pos


def put_keys(kt, start, keys, first_pixel):
    count = keys.shape[0]
    cols = pl.ds(start, count)
    kt[0:CH, cols] = keys.T
    row = lax.broadcasted_iota(jnp.int32, (16, count), 0)
    pixel = first_pixel + lax.broadcasted_iota(jnp.int32, (16, count), 1)
    column_pos, row_pos = grid_xy(pixel)
    extra = jnp.where(row == 0, column_pos, jnp.where(row == 1, row_pos, jnp.where(row == 2, 1.0, 0.0)))
    kt[CH:AUG, cols] = extra.astype(BF16)


def attend(queries, keys, kt, scores):
    count = keys.shape[0]
    scores[0:count, :] = lax.dot_general(
        keys, queries, (((1,), (1,)), ((), ())), preferred_element_type=F32
    )
    peak = jnp.max(scores[0:count, :], axis=0, keepdims=True)
    weights = jnp.exp2((scores[0:count, :] - peak) * SCALE).astype(BF16)
    total = jnp.dot(kt, weights, preferred_element_type=F32)
    row = lax.broadcasted_iota(jnp.int32, (8, CHUNK), 0)
    return total[0:CH], jnp.where(row == 3, peak, total[CH:MSG])


def merge(parts):
    peaks = [extra[3:4] for _, extra in parts]
    peak = functools.reduce(jnp.maximum, peaks)
    gains = [jnp.exp2((p - peak) * SCALE) for p in peaks]
    feat = sum(f * g for (f, _), g in zip(parts, gains))
    extra = sum(e * g for (_, e), g in zip(parts, gains))
    row = lax.broadcasted_iota(jnp.int32, extra.shape, 0)
    return feat, jnp.where(row == 3, peak, extra)


def pack(feat, extra, out):
    low_lane = lax.broadcasted_iota(jnp.int32, (PART, CH), 1) < PART
    low_extra = lax.broadcasted_iota(jnp.int32, (8, CH), 1) < PART
    for t in range(2):
        low, high = feat[0:PART, t * CH:(t + 1) * CH], feat[PART:CH, t * CH:(t + 1) * CH]
        ext = extra[:, t * CH:(t + 1) * CH]
        ext_roll = pltpu.roll(ext, PART, 1)
        out[2 * t, 0:PART] = jnp.where(low_lane, low, pltpu.roll(high, PART, 1))
        out[2 * t, PART:PACK] = jnp.where(low_extra, ext, ext_roll)
        out[2 * t + 1, 0:PART] = jnp.where(low_lane, pltpu.roll(low, PART, 1), high)
        out[2 * t + 1, PART:PACK] = jnp.where(low_extra, ext_roll, ext)


def finish(parts, first_pixel, warped, flow):
    feat, extra = merge(parts)
    inverse = 1.0 / extra[2:3]
    turned = (feat * inverse).T
    warped[:, 0:PART] = turned[0:PART]
    warped[:, PART:CH] = turned[PART:CH]
    pixel = first_pixel + lax.broadcasted_iota(jnp.int32, (1, PART), 1)
    column_pos, row_pos = grid_xy(pixel)
    coord = (extra * inverse)[:, 0:PART]
    flow[0:1] = coord[0:1] - column_pos
    flow[1:2] = coord[1:2] - row_pos


def kernel(
    f1, f2, warped_one, flow_one, warped_two, flow_two,
    sent_keys, got_keys, keys_one, kt_one, kt_two, scores,
    a1_out, a1_in, b1_out, b1_in, a2_out, a2_in, b2_out, b2_in,
    core_send, core_recv, a1_send, a1_recv, b1_send, b1_recv,
    a2_send, a2_recv, b2_send, b2_recv,
):
    aa, ba = lax.axis_index("aa"), lax.axis_index("ba")
    core = lax.rem(aa, 2)
    z = lax.rem(lax.div(aa, 2), 8)
    y_lo = lax.div(aa, 16)
    z_hi, z_lo = lax.div(z, 2), lax.rem(z, 2)
    x, y_hi = lax.div(ba, 4), lax.rem(ba, 4)
    group = y_lo * 2 + z_lo
    rows_one = f1.shape[0]

    def turn(value, offset):
        return lax.rem(value + offset, 4)

    def a1_peer(offset):
        return (aa, turn(x, offset) * 4 + y_hi)

    def a2_peer(offset):
        return (aa, x * 4 + turn(y_hi, offset))

    def b1_peer(offset):
        to = turn(group, offset)
        return ((lax.div(to, 2) * 8 + z_hi * 2 + lax.rem(to, 2)) * 2 + core, ba)

    def b2_peer(offset):
        return ((y_lo * 8 + turn(z_hi, offset) * 2 + z_lo) * 2 + core, ba)

    sibling = (aa + 1 - 2 * core, ba)

    def remote(src, dst, send, recv, peer):
        return pltpu.make_async_remote_copy(
            src_ref=src, dst_ref=dst, send_sem=send, recv_sem=recv, device_id=peer, device_id_type=MESH
        )

    def a1_copy(s):
        return remote(a1_out.at[s], a1_in.at[s], a1_send.at[s], a1_recv.at[s], a1_peer(s + 1))

    def b1_copy(s):
        return remote(b1_out.at[s], b1_in.at[s], b1_send.at[s], b1_recv.at[s], b1_peer(s + 1))

    def a2_copy(s):
        return remote(
            a2_out.at[turn(y_hi, s + 1)], a2_in.at[s], a2_send.at[s], a2_recv.at[s], a2_peer(s + 1)
        )

    def b2_copy(s):
        return remote(
            b2_out.at[turn(z_hi, s + 1)], b2_in.at[s], b2_send.at[s], b2_recv.at[s], b2_peer(s + 1)
        )

    barrier = pltpu.get_barrier_semaphore()
    for peers in (a1_peer, a2_peer, b1_peer, b2_peer):
        for s in range(3):
            pl.semaphore_signal(barrier, inc=1, device_id=peers(s + 1), device_id_type=MESH)
    pl.semaphore_signal(barrier, inc=1, device_id=sibling, device_id_type=MESH)

    sent_keys[...] = f1[...].astype(F32)
    put_keys(kt_two, 0, f2[...], ba * f2.shape[0])

    def a_chunk(s):
        start = pl.multiple_of(turn(x, s + 1) * CHUNK, CHUNK)
        feat, extra = attend(f1[pl.ds(start, CHUNK)], f2[...], kt_two[...], scores)
        a1_out[s, 0:CH] = feat
        a1_out[s, CH:MSG] = extra

    def b_queries(s):
        to = turn(group, s + 1)
        first = lax.div(to, 2) * 8 + lax.rem(to, 2)
        blocks = []
        for j in range(4):
            start = pl.multiple_of(((first + 2 * j) * 2 + core) * PART, PART)
            blocks.append(f2[pl.ds(start, PART)])
        return jnp.concatenate(blocks, axis=0)

    def a_early(s, carry):
        a_chunk(s)
        return carry

    lax.fori_loop(0, 2, a_early, 0)
    pl.semaphore_wait(barrier, 13)
    keys_copy = remote(sent_keys, got_keys, core_send, core_recv, sibling)
    keys_copy.start()
    a1_copy(0).start()
    a1_copy(1).start()

    def a_late(s, carry):
        a_chunk(s)

        @pl.when(s < 3)
        def _():
            a1_copy(s).start()

        return carry

    lax.fori_loop(2, 4, a_late, 0)

    put_keys(kt_one, 0, f1[...], aa * rows_one)

    def b_early(s, carry):
        feat, extra = attend(b_queries(s), f1[...], kt_one[:, 0:rows_one], scores)
        b1_out[s, 0:CH] = feat
        b1_out[s, CH:MSG] = extra
        return carry

    lax.fori_loop(0, 4, b_early, 0)

    keys_copy.wait_recv()
    keys_one[...] = got_keys[...].astype(BF16)
    put_keys(kt_one, rows_one, keys_one[...], sibling[0] * rows_one)

    def b_late(s, carry):
        part = attend(
            b_queries(s), keys_one[...], kt_one[:, rows_one:2 * rows_one], scores
        )
        feat, extra = merge([(b1_out[s, 0:CH], b1_out[s, CH:MSG]), part])
        b1_out[s, 0:CH] = feat
        b1_out[s, CH:MSG] = extra

        @pl.when(s < 3)
        def _():
            b1_copy(s).start()

        return carry

    lax.fori_loop(0, 4, b_late, 0)

    def first_merge(own, got, out):
        parts = [(own[3, 0:CH], own[3, CH:MSG])]
        parts += [(got[s, 0:CH], got[s, CH:MSG]) for s in range(3)]
        feat, extra = merge(parts)
        pack(feat, extra, out)

    def last_merge(mine, out, got, first_pixel, warped, flow):
        parts = [(out[mine, 0:PART], out[mine, PART:PACK])]
        parts += [(got[s, 0:PART], got[s, PART:PACK]) for s in range(3)]
        finish(parts, first_pixel, warped, flow)

    for s in range(3):
        a1_copy(s).wait_recv()
    first_merge(a1_out, a1_in, a2_out)
    for s in range(3):
        a2_copy(s).start()
    for s in range(3):
        b1_copy(s).wait_recv()
    first_merge(b1_out, b1_in, b2_out)
    for s in range(3):
        b2_copy(s).start()
    for s in range(3):
        a2_copy(s).wait_recv()
    last_merge(y_hi, a2_out, a2_in, (aa * 16 + ba) * PART, warped_one, flow_one)
    for s in range(3):
        b2_copy(s).wait_recv()
    last_merge(z_hi, b2_out, b2_in, (ba * 32 + aa) * PART, warped_two, flow_two)

    keys_copy.wait_send()
    for s in range(3):
        a1_copy(s).wait_send()
        b1_copy(s).wait_send()
        a2_copy(s).wait_send()
        b2_copy(s).wait_send()


def shards(frame_one, frame_two):
    rows_one, rows_two = frame_one.shape[0], frame_two.shape[0]
    vmem = pl.BlockSpec(memory_space=pltpu.VMEM)
    dma = pltpu.SemaphoreType.DMA
    return pl.pallas_call(
        kernel,
        out_shape=(
            jax.ShapeDtypeStruct((PART, CH), F32),
            jax.ShapeDtypeStruct((2, PART), F32),
            jax.ShapeDtypeStruct((PART, CH), F32),
            jax.ShapeDtypeStruct((2, PART), F32),
        ),
        in_specs=[vmem, vmem],
        out_specs=(vmem,) * 4,
        scratch_shapes=[
            pltpu.VMEM((rows_one, CH), F32),
            pltpu.VMEM((rows_one, CH), F32),
            pltpu.VMEM((rows_one, CH), BF16),
            pltpu.VMEM((AUG, 2 * rows_one), BF16),
            pltpu.VMEM((AUG, rows_two), BF16),
            pltpu.VMEM((rows_two, CHUNK), F32),
            pltpu.VMEM((4, MSG, CHUNK), F32),
            pltpu.VMEM((3, MSG, CHUNK), F32),
            pltpu.VMEM((4, MSG, CHUNK), F32),
            pltpu.VMEM((3, MSG, CHUNK), F32),
            pltpu.VMEM((4, PACK, CH), F32),
            pltpu.VMEM((3, PACK, CH), F32),
            pltpu.VMEM((4, PACK, CH), F32),
            pltpu.VMEM((3, PACK, CH), F32),
            dma, dma,
            dma((3,)), dma((3,)), dma((3,)), dma((3,)),
            dma((3,)), dma((3,)), dma((3,)), dma((3,)),
        ],
        compiler_params=pltpu.CompilerParams(
            collective_id=0, has_side_effects=True, vmem_limit_bytes=40 * 1024 * 1024
        ),
        name="match",
    )(frame_one, frame_two)


def solution(mesh):
    return jax.shard_map(
        shards,
        mesh=mesh,
        in_specs=(P("aa", None), P("ba", None)),
        out_specs=(
            P(("aa", "ba"), None),
            P(None, ("aa", "ba")),
            P(("ba", "aa"), None),
            P(None, ("ba", "aa")),
        ),
        check_vma=False,
    )
```

```python
import functools
import math

import jax
import jax.numpy as jnp
from jax import lax
from jax.experimental import pallas as pl
from jax.experimental.pallas import tpu as pltpu
from jax.sharding import PartitionSpec as P

IMG_W = 128
CH = 128
MSG = CH + 8
AUG = CH + 16
CHUNK = 256
PART = 64
PACK = PART + 8
TILE = 512
SCALE = CH ** (-0.5) * math.log2(math.e)
MESH = pl.DeviceIdType.MESH
A_ORDER = (2, 1, 3, 0)
B_ORDER = (3, 2, 1, 0)
F32 = jnp.float32
BF16 = jnp.bfloat16


def grid_xy(pixel):
    column_pos = lax.rem(pixel, IMG_W).astype(F32) / 64.0
    row_pos = lax.div(pixel, IMG_W).astype(F32) / 64.0
    return column_pos, row_pos


def put_keys(kt, start, keys, first_pixel):
    count = keys.shape[0]
    cols = pl.ds(start, count)
    kt[0:CH, cols] = keys.T
    row = lax.broadcasted_iota(jnp.int32, (16, count), 0)
    pixel = first_pixel + lax.broadcasted_iota(jnp.int32, (16, count), 1)
    column_pos, row_pos = grid_xy(pixel)
    extra = jnp.where(row == 0, column_pos, jnp.where(row == 1, row_pos, jnp.where(row == 2, 1.0, 0.0)))
    kt[CH:AUG, cols] = extra.astype(BF16)


def score_steps(queries, keys, scores, peaks):
    def step(first):
        rows = slice(first, first + TILE)
        tile = lax.dot_general(
            keys[rows], queries, (((1,), (1,)), ((), ())), preferred_element_type=F32
        )
        scores[rows] = tile
        peaks.append(jnp.max(tile.reshape(TILE // 8, 8, CHUNK), axis=0))

    return [functools.partial(step, first) for first in range(0, keys.shape[0], TILE)]


def sum_steps(kt, scores, peak, sums):
    def step(first):
        cols = slice(first, first + TILE)
        weights = jnp.exp2((scores[cols] - peak) * SCALE).astype(BF16)
        sums.append(jnp.dot(kt[:, cols], weights, preferred_element_type=F32))

    return [functools.partial(step, first) for first in range(0, kt.shape[1], TILE)]


def attend(units, scores):
    peaks = []
    for step in score_steps(units[0][0](), units[0][1], scores[0], peaks):
        step()
    for i, (_, _, kt, use) in enumerate(units):
        peak = jnp.max(functools.reduce(jnp.maximum, peaks), axis=0, keepdims=True)
        sums, peaks = [], []
        ahead = []
        if i + 1 < len(units):
            ahead = score_steps(units[i + 1][0](), units[i + 1][1], scores[(i + 1) % 2], peaks)
        now = sum_steps(kt, scores[i % 2], peak, sums)
        for j in range(max(len(ahead), len(now))):
            for steps in (ahead, now):
                if j < len(steps):
                    steps[j]()
        total = functools.reduce(jnp.add, sums)
        row = lax.broadcasted_iota(jnp.int32, (8, CHUNK), 0)
        use(total[0:CH], jnp.where(row == 3, peak, total[CH:MSG]))


def merge(parts):
    peaks = [extra[3:4] for _, extra in parts]
    peak = functools.reduce(jnp.maximum, peaks)
    gains = [jnp.exp2((p - peak) * SCALE) for p in peaks]
    feat = sum(f * g for (f, _), g in zip(parts, gains))
    extra = sum(e * g for (_, e), g in zip(parts, gains))
    row = lax.broadcasted_iota(jnp.int32, extra.shape, 0)
    return feat, jnp.where(row == 3, peak, extra)


def pack(feat, extra, out):
    low_lane = lax.broadcasted_iota(jnp.int32, (PART, CH), 1) < PART
    low_extra = lax.broadcasted_iota(jnp.int32, (8, CH), 1) < PART
    for t in range(2):
        low, high = feat[0:PART, t * CH:(t + 1) * CH], feat[PART:CH, t * CH:(t + 1) * CH]
        ext = extra[:, t * CH:(t + 1) * CH]
        ext_roll = pltpu.roll(ext, PART, 1)
        out[2 * t, 0:PART] = jnp.where(low_lane, low, pltpu.roll(high, PART, 1))
        out[2 * t, PART:PACK] = jnp.where(low_extra, ext, ext_roll)
        out[2 * t + 1, 0:PART] = jnp.where(low_lane, pltpu.roll(low, PART, 1), high)
        out[2 * t + 1, PART:PACK] = jnp.where(low_extra, ext_roll, ext)


def finish(parts, first_pixel, warped, flow):
    feat, extra = merge(parts)
    inverse = 1.0 / extra[2:3]
    turned = (feat * inverse).T
    warped[:, 0:PART] = turned[0:PART]
    warped[:, PART:CH] = turned[PART:CH]
    pixel = first_pixel + lax.broadcasted_iota(jnp.int32, (1, PART), 1)
    column_pos, row_pos = grid_xy(pixel)
    coord = (extra * inverse)[:, 0:PART]
    flow[0:1] = coord[0:1] - column_pos
    flow[1:2] = coord[1:2] - row_pos


def kernel(
    f1_hbm, f2_hbm, warped_one, flow_one, warped_two, flow_two,
    f1, f2, kt_one, kt_two, scores_even, scores_odd,
    core_out, core_in, a1_out, a1_in, b1_out, b1_in, a2_out, a2_in, b2_out, b2_in,
    load, core_send, core_recv, a1_send, a1_recv, b1_send, b1_recv,
    a2_send, a2_recv, b2_send, b2_recv,
):
    load_one = pltpu.make_async_copy(f1_hbm, f1, load.at[0])
    load_two = pltpu.make_async_copy(f2_hbm, f2, load.at[1])
    load_one.start()
    load_two.start()

    aa, ba = lax.axis_index("aa"), lax.axis_index("ba")
    core = lax.rem(aa, 2)
    z = lax.rem(lax.div(aa, 2), 8)
    y_lo = lax.div(aa, 16)
    z_hi, z_lo = lax.div(z, 2), lax.rem(z, 2)
    x, y_hi = lax.div(ba, 4), lax.rem(ba, 4)

    def turn(value, offset):
        return lax.rem(value + offset, 4)

    def a1_peer(offset):
        return (aa, turn(x, offset) * 4 + y_hi)

    def a2_peer(offset):
        return (aa, x * 4 + turn(y_hi, offset))

    def b1_block(offset):
        return lax.rem(y_lo + offset // 2, 2) * 8 + lax.rem(z_lo + offset % 2, 2)

    def b1_peer(offset):
        return ((b1_block(offset) + z_hi * 2) * 2 + core, ba)

    def b2_peer(offset):
        return ((y_lo * 8 + turn(z_hi, offset) * 2 + z_lo) * 2 + core, ba)

    sibling = (aa + 1 - 2 * core, ba)

    def remote(src, dst, sems, slot, peer):
        return pltpu.make_async_remote_copy(
            src_ref=src, dst_ref=dst.at[slot], send_sem=sems[0].at[slot], recv_sem=sems[1].at[slot],
            device_id=peer, device_id_type=MESH,
        )

    core_copy = [
        remote(core_out.at[s], core_in, (core_send, core_recv), s, sibling) for s in range(4)
    ]
    a1_copy = {
        s: remote(a1_out.at[s], a1_in, (a1_send, a1_recv), s - 1, a1_peer(s)) for s in (1, 2, 3)
    }
    b1_copy = {
        s: remote(b1_out.at[s], b1_in, (b1_send, b1_recv), s - 1, b1_peer(s)) for s in (1, 2, 3)
    }
    a2_copy = {
        s: remote(a2_out.at[turn(y_hi, s)], a2_in, (a2_send, a2_recv), s - 1, a2_peer(s))
        for s in (1, 2, 3)
    }
    b2_copy = {
        s: remote(b2_out.at[turn(z_hi, s)], b2_in, (b2_send, b2_recv), s - 1, b2_peer(s))
        for s in (1, 2, 3)
    }

    barrier = pltpu.get_barrier_semaphore()
    for s in (2, 1, 3):
        for peers in (a2_peer, b2_peer, a1_peer, b1_peer):
            pl.semaphore_signal(barrier, inc=1, device_id=peers(s), device_id_type=MESH)
    pl.semaphore_signal(barrier, inc=1, device_id=sibling, device_id_type=MESH)

    load_one.wait()
    put_keys(kt_one, 0, f1[...], aa * f1.shape[0])
    load_two.wait()
    put_keys(kt_two, 0, f2[...], ba * f2.shape[0])

    def a_queries(offset):
        start = pl.multiple_of(turn(x, offset) * CHUNK, CHUNK)
        return f1[pl.ds(start, CHUNK)]

    def b_queries(offset, parity):
        blocks = []
        for j in range(4):
            start = pl.multiple_of(((b1_block(offset) + 2 * j) * 2 + parity) * PART, PART)
            blocks.append(f2[pl.ds(start, PART)])
        return jnp.concatenate(blocks, axis=0)

    def put(out):
        def use(feat, extra):
            out[0:CH] = feat
            out[CH:MSG] = extra

        return use

    def share(offset):
        core_copy[offset].wait_recv()
        mine, got = b1_out.at[offset], core_in.at[offset]
        feat, extra = merge([(mine[0:CH], mine[CH:MSG]), (got[0:CH], got[CH:MSG])])
        put(mine)(feat, extra)
        if offset:
            b1_copy[offset].start()

    def a_use(offset, shared):
        def use(feat, extra):
            if offset == A_ORDER[0]:
                pl.semaphore_wait(barrier, 13)
                for s in B_ORDER:
                    core_copy[s].start()
            put(a1_out.at[offset])(feat, extra)
            if offset:
                a1_copy[offset].start()
            for s in shared:
                share(s)

        return use

    units = [
        (functools.partial(b_queries, s, 1 - core), f1, kt_one, put(core_out.at[s])) for s in B_ORDER
    ]
    units += [
        (functools.partial(b_queries, s, core), f1, kt_one, put(b1_out.at[s])) for s in B_ORDER
    ]
    units += [
        (functools.partial(a_queries, s), f2, kt_two, a_use(s, shared))
        for s, shared in zip(A_ORDER, ((), B_ORDER[0:1], B_ORDER[1:3], B_ORDER[3:4]))
    ]
    attend(units, (scores_even, scores_odd))

    def first_merge(own, got, out):
        parts = [(own[0, 0:CH], own[0, CH:MSG])]
        parts += [(got[s, 0:CH], got[s, CH:MSG]) for s in range(3)]
        feat, extra = merge(parts)
        pack(feat, extra, out)

    def last_merge(mine, out, got, first_pixel, warped, flow):
        parts = [(out[mine, 0:PART], out[mine, PART:PACK])]
        parts += [(got[s, 0:PART], got[s, PART:PACK]) for s in range(3)]
        finish(parts, first_pixel, warped, flow)

    def wait_all(copies):
        for s in (1, 2, 3):
            copies[s].wait_recv()

    def start_all(copies):
        for s in (2, 1, 3):
            copies[s].start()

    wait_all(a1_copy)
    first_merge(a1_out, a1_in, a2_out)
    start_all(a2_copy)
    wait_all(b1_copy)
    first_merge(b1_out, b1_in, b2_out)
    start_all(b2_copy)
    wait_all(a2_copy)
    last_merge(y_hi, a2_out, a2_in, (aa * 16 + ba) * PART, warped_one, flow_one)
    wait_all(b2_copy)
    last_merge(z_hi, b2_out, b2_in, (ba * 32 + aa) * PART, warped_two, flow_two)

    for s in range(4):
        core_copy[s].wait_send()
    for copies in (a1_copy, b1_copy, a2_copy, b2_copy):
        for s in (1, 2, 3):
            copies[s].wait_send()


def emit(w1, g1, w2, g2, warped_one, flow_one, warped_two, flow_two, done):
    pairs = ((w1, warped_one), (g1, flow_one), (w2, warped_two), (g2, flow_two))
    copies = [pltpu.make_async_copy(src, dst, done.at[i]) for i, (src, dst) in enumerate(pairs)]
    for copy in copies:
        copy.start()
    for copy in copies:
        copy.wait()


def shards(frame_one, frame_two):
    rows_one, rows_two = frame_one.shape[0], frame_two.shape[0]
    vmem = pl.BlockSpec(memory_space=pltpu.VMEM)
    hbm = pl.BlockSpec(memory_space=pltpu.HBM)
    dma = pltpu.SemaphoreType.DMA
    shapes = (
        jax.ShapeDtypeStruct((PART, CH), F32),
        jax.ShapeDtypeStruct((2, PART), F32),
        jax.ShapeDtypeStruct((PART, CH), F32),
        jax.ShapeDtypeStruct((2, PART), F32),
    )
    results = pl.pallas_call(
        kernel,
        out_shape=shapes,
        in_specs=[hbm, hbm],
        out_specs=(vmem,) * 4,
        scratch_shapes=[
            pltpu.VMEM((rows_one, CH), BF16),
            pltpu.VMEM((rows_two, CH), BF16),
            pltpu.VMEM((AUG, rows_one), BF16),
            pltpu.VMEM((AUG, rows_two), BF16),
            pltpu.VMEM((rows_two, CHUNK), F32),
            pltpu.VMEM((rows_two, CHUNK), F32),
            pltpu.VMEM((4, MSG, CHUNK), F32),
            pltpu.VMEM((4, MSG, CHUNK), F32),
            pltpu.VMEM((4, MSG, CHUNK), F32),
            pltpu.VMEM((3, MSG, CHUNK), F32),
            pltpu.VMEM((4, MSG, CHUNK), F32),
            pltpu.VMEM((3, MSG, CHUNK), F32),
            pltpu.VMEM((4, PACK, CH), F32),
            pltpu.VMEM((3, PACK, CH), F32),
            pltpu.VMEM((4, PACK, CH), F32),
            pltpu.VMEM((3, PACK, CH), F32),
            dma((2,)),
            dma((4,)), dma((4,)),
            dma((3,)), dma((3,)), dma((3,)), dma((3,)),
            dma((3,)), dma((3,)), dma((3,)), dma((3,)),
        ],
        compiler_params=pltpu.CompilerParams(
            collective_id=0, has_side_effects=True, vmem_limit_bytes=54976 * 1024
        ),
        name="match",
    )(frame_one, frame_two)
    return pl.pallas_call(
        emit,
        out_shape=shapes,
        in_specs=[vmem] * 4,
        out_specs=(hbm,) * 4,
        scratch_shapes=[dma((4,))],
        compiler_params=pltpu.CompilerParams(vmem_limit_bytes=1024 * 1024),
        name="emit",
    )(*results)


def solution(mesh):
    return jax.shard_map(
        shards,
        mesh=mesh,
        in_specs=(P("aa", None), P("ba", None)),
        out_specs=(
            P(("aa", "ba"), None),
            P(None, ("aa", "ba")),
            P(("ba", "aa"), None),
            P(None, ("ba", "aa")),
        ),
        check_vma=False,
    )
```

```python
import functools
import math

import jax
import jax.numpy as jnp
from jax import lax
from jax.experimental import pallas as pl
from jax.experimental.pallas import tpu as pltpu
from jax.sharding import PartitionSpec as P

IMG_W = 128
CH = 128
MSG = CH + 8
AUG = CH + 16
CHUNK = 256
PART = 64
PACK = PART + 8
TILE = 512
SCALE = CH ** (-0.5) * math.log2(math.e)
MESH = pl.DeviceIdType.MESH
Y_SLOTS = ((0, 1), (3, 2))
Z_SLOTS = ((0, 1), (2, 3))
F32 = jnp.float32
BF16 = jnp.bfloat16


def grid_xy(pixel):
    column_pos = lax.rem(pixel, IMG_W).astype(F32) / 64.0
    row_pos = lax.div(pixel, IMG_W).astype(F32) / 64.0
    return column_pos, row_pos


def put_keys(kt, start, keys, first_pixel):
    count = keys.shape[0]
    cols = pl.ds(start, count)
    kt[0:CH, cols] = keys.T
    row = lax.broadcasted_iota(jnp.int32, (16, count), 0)
    pixel = first_pixel + lax.broadcasted_iota(jnp.int32, (16, count), 1)
    column_pos, row_pos = grid_xy(pixel)
    extra = jnp.where(row == 0, column_pos, jnp.where(row == 1, row_pos, jnp.where(row == 2, 1.0, 0.0)))
    kt[CH:AUG, cols] = extra.astype(BF16)


def score_steps(queries, keys, scores, peaks):
    def step(first):
        rows = slice(first, first + TILE)
        tile = lax.dot_general(
            keys[rows], queries, (((1,), (1,)), ((), ())), preferred_element_type=F32
        )
        scores[rows] = tile
        peaks.append(jnp.max(tile.reshape(TILE // 8, 8, CHUNK), axis=0))

    return [functools.partial(step, first) for first in range(0, keys.shape[0], TILE)]


def sum_steps(kt, scores, peak, sums):
    def step(first):
        cols = slice(first, first + TILE)
        weights = jnp.exp2((scores[cols] - peak) * SCALE).astype(BF16)
        sums.append(jnp.dot(kt[:, cols], weights, preferred_element_type=F32))

    return [functools.partial(step, first) for first in range(0, kt.shape[1], TILE)]


def attend(units, scores):
    peaks = []
    for step in score_steps(units[0][0](), units[0][1], scores[0], peaks):
        step()
    for i, (_, _, kt, use) in enumerate(units):
        peak = jnp.max(functools.reduce(jnp.maximum, peaks), axis=0, keepdims=True)
        sums, peaks = [], []
        ahead = []
        if i + 1 < len(units):
            ahead = score_steps(units[i + 1][0](), units[i + 1][1], scores[(i + 1) % 2], peaks)
        now = sum_steps(kt, scores[i % 2], peak, sums)
        for j in range(max(len(ahead), len(now))):
            for steps in (ahead, now):
                if j < len(steps):
                    steps[j]()
        total = functools.reduce(jnp.add, sums)
        row = lax.broadcasted_iota(jnp.int32, (8, CHUNK), 0)
        use(total[0:CH], jnp.where(row == 3, peak, total[CH:MSG]))


def merge(parts):
    peaks = [extra[3:4] for _, extra in parts]
    peak = functools.reduce(jnp.maximum, peaks)
    gains = [jnp.exp2((p - peak) * SCALE) for p in peaks]
    feat = sum(f * g for (f, _), g in zip(parts, gains))
    extra = sum(e * g for (_, e), g in zip(parts, gains))
    row = lax.broadcasted_iota(jnp.int32, extra.shape, 0)
    return feat, jnp.where(row == 3, peak, extra)


def pack(feat, extra, out, slots):
    low_lane = lax.broadcasted_iota(jnp.int32, (PART, CH), 1) < PART
    low_extra = lax.broadcasted_iota(jnp.int32, (8, CH), 1) < PART
    low, high = feat[0:PART], feat[PART:CH]
    turned = pltpu.roll(extra, PART, 1)
    out[slots[0], 0:PART] = jnp.where(low_lane, low, pltpu.roll(high, PART, 1))
    out[slots[0], PART:PACK] = jnp.where(low_extra, extra, turned)
    out[slots[1], 0:PART] = jnp.where(low_lane, pltpu.roll(low, PART, 1), high)
    out[slots[1], PART:PACK] = jnp.where(low_extra, turned, extra)


def finish(parts, first_pixel, warped, flow):
    feat, extra = merge(parts)
    inverse = 1.0 / extra[2:3]
    turned = (feat * inverse).T
    warped[:, 0:PART] = turned[0:PART]
    warped[:, PART:CH] = turned[PART:CH]
    pixel = first_pixel + lax.broadcasted_iota(jnp.int32, (1, PART), 1)
    column_pos, row_pos = grid_xy(pixel)
    coord = (extra * inverse)[:, 0:PART]
    flow[0:1] = coord[0:1] - column_pos
    flow[1:2] = coord[1:2] - row_pos


class Group:
    def __init__(self, rank, peer, out, got, sems):
        self.rank, self.peer, self.out, self.got = rank, peer, out, got
        self.send_sem, self.recv_sem = sems

    def others(self):
        return [lax.rem(self.rank + t, 4) for t in range(1, 4)]

    def greet(self, barrier):
        for k in self.others():
            pl.semaphore_signal(barrier, inc=1, device_id=self.peer(k), device_id_type=MESH)

    def copy(self, k, half=0):
        to, mine = 4 * half + k, 4 * half + self.rank
        return pltpu.make_async_remote_copy(
            src_ref=self.out.at[to], dst_ref=self.got.at[mine],
            send_sem=self.send_sem.at[to], recv_sem=self.recv_sem.at[mine],
            device_id=self.peer(k), device_id_type=MESH,
        )

    def send(self, k, half=0):
        @pl.when(k != self.rank)
        def _():
            self.copy(k, half).start()

    def wait_recv(self, half=0):
        for k in self.others():
            slot = 4 * half + k
            pltpu.make_async_remote_copy(
                src_ref=self.out.at[slot], dst_ref=self.got.at[slot],
                send_sem=self.send_sem.at[slot], recv_sem=self.recv_sem.at[slot],
                device_id=self.peer(k), device_id_type=MESH,
            ).wait_recv()

    def wait_send(self, half=0):
        for k in self.others():
            self.copy(k, half).wait_send()

    def parts(self, rows, half=0):
        own = self.out.at[4 * half + self.rank]
        parts = [(own[0:rows], own[rows:rows + 8])]
        for k in self.others():
            got = self.got.at[4 * half + k]
            parts.append((got[0:rows], got[rows:rows + 8]))
        return parts


class RankedGroup(Group):
    def __init__(self, rank, peer, out, got, sems):
        super().__init__(rank, peer, out, got, sems[0:2])
        self.ready = sems[2]

    def greet(self, barrier):
        for k in range(4):
            @pl.when(k > self.rank)
            def _():
                pl.semaphore_signal(barrier, inc=1, device_id=self.peer(k), device_id_type=MESH)

    def answer(self):
        for k in range(4):
            @pl.when(k < self.rank)
            def _():
                pl.semaphore_signal(
                    self.ready.at[self.rank], inc=1, device_id=self.peer(k), device_id_type=MESH
                )

    def send(self, k, half=0):
        @pl.when(k < self.rank)
        def _():
            self.copy(k).start()

        @pl.when(k > self.rank)
        def _():
            pl.semaphore_wait(self.ready.at[k], 1)
            self.copy(k).start()


def kernel(
    f1_hbm, f2_hbm, warped_one, flow_one, warped_two, flow_two,
    f1, f2, kt_one, kt_two, scores_even, scores_odd,
    core_out, core_in, core_own, x_out, x_in, w_out, w_in, y_out, y_in, z_out, z_in,
    load, core_send, core_recv, x_send, x_recv, w_send, w_recv, y_send, y_recv, z_send, z_recv,
    y_ready, z_ready,
):
    load_one = pltpu.make_async_copy(f1_hbm, f1, load.at[0])
    load_two = pltpu.make_async_copy(f2_hbm, f2, load.at[1])
    load_one.start()
    load_two.start()

    aa, ba = lax.axis_index("aa"), lax.axis_index("ba")
    core = lax.rem(aa, 2)
    z = lax.rem(lax.div(aa, 2), 8)
    y_lo = lax.div(aa, 16)
    z_hi, z_lo = lax.div(z, 2), lax.rem(z, 2)
    x, y_hi = lax.div(ba, 4), lax.rem(ba, 4)

    def y_slot(value):
        return value + lax.div(value, 2) * (5 - 2 * value)

    sibling = (aa + 1 - 2 * core, ba)
    x_group = Group(x, lambda k: (aa, k * 4 + y_hi), x_out, x_in, (x_send, x_recv))
    w_group = Group(
        y_lo * 2 + z_lo,
        lambda k: ((lax.div(k, 2) * 8 + z_hi * 2 + lax.rem(k, 2)) * 2 + core, ba),
        w_out, w_in, (w_send, w_recv),
    )
    y_group = RankedGroup(
        y_slot(y_hi), lambda k: (aa, x * 4 + y_slot(k)), y_out, y_in, (y_send, y_recv, y_ready)
    )
    z_group = RankedGroup(
        z_hi, lambda k: ((y_lo * 8 + k * 2 + z_lo) * 2 + core, ba), z_out, z_in, (z_send, z_recv, z_ready)
    )

    barrier = pltpu.get_barrier_semaphore()
    pl.semaphore_signal(barrier, inc=1, device_id=sibling, device_id_type=MESH)
    for group in (w_group, x_group, z_group, y_group):
        group.greet(barrier)

    load_one.wait()
    put_keys(kt_one, 0, f1[...], aa * f1.shape[0])
    load_two.wait()

    core_copy = [
        pltpu.make_async_remote_copy(
            src_ref=core_out.at[u], dst_ref=core_in.at[u],
            send_sem=core_send.at[u], recv_sem=core_recv.at[u],
            device_id=sibling, device_id_type=MESH,
        )
        for u in range(4)
    ]

    def b_queries(half, pair, parity):
        blocks = []
        for k in (2 * pair, 2 * pair + 1):
            for j in (2 * half, 2 * half + 1):
                block = (k // 2) * 8 + 2 * j + k % 2
                start = pl.multiple_of((block * 2 + parity) * PART, PART)
                blocks.append(f2[pl.ds(start, PART)])
        return jnp.concatenate(blocks, axis=0)

    def a_queries(half, pair):
        starts = [k * CHUNK + half * CH for k in (2 * pair, 2 * pair + 1)]
        return jnp.concatenate([f1[start:start + CH] for start in starts], axis=0)

    def put(out, feat, extra):
        out[0:CH] = feat
        out[CH:MSG] = extra

    def split(out, half, pair, feat, extra):
        for t in range(2):
            lanes = slice(t * CH, (t + 1) * CH)
            put(out.at[4 * half + 2 * pair + t], feat[:, lanes], extra[:, lanes])

    def enter():
        pl.semaphore_wait(barrier, 7 + y_group.rank + z_group.rank)
        core_copy[0].start()
        core_copy[1].start()
        z_group.answer()
        y_group.answer()

    def share(half, pair):
        u = 2 * half + pair
        core_copy[u].wait_recv()
        mine, got = core_own.at[u], core_in.at[u]
        feat, extra = merge([(mine[0:CH], mine[CH:MSG]), (got[0:CH], got[CH:MSG])])
        split(w_out, half, pair, feat, extra)
        for k in (2 * pair, 2 * pair + 1):
            w_group.send(k, half)

    def second(first_group, second_group, half, slots):
        first_group.wait_recv(half)
        feat, extra = merge(first_group.parts(CH, half))
        pack(feat, extra, second_group.out, slots[half])
        for k in (2 * half, 2 * half + 1):
            second_group.send(k)

    def b_other(half, pair, after=()):
        def use(feat, extra):
            u = 2 * half + pair
            put(core_out.at[u], feat, extra)
            if half:
                core_copy[u].start()
            for step in after:
                step()

        return functools.partial(b_queries, half, pair, 1 - core), f1, kt_one, use

    def b_own(half, pair, after=()):
        def use(feat, extra):
            put(core_own.at[2 * half + pair], feat, extra)
            for step in after:
                step()

        return functools.partial(b_queries, half, pair, core), f1, kt_one, use

    def a_unit(half, pair, after=()):
        def use(feat, extra):
            split(x_out, half, pair, feat, extra)
            for k in (2 * pair, 2 * pair + 1):
                x_group.send(k, half)
            for step in after:
                step()

        return functools.partial(a_queries, half, pair), f2, kt_two, use

    def late_keys():
        put_keys(kt_two, 0, f2[...], ba * f2.shape[0])

    attend(
        [
            b_other(0, 0), b_other(0, 1, (enter,)), b_own(0, 0, (late_keys,)), b_own(0, 1),
            a_unit(0, 0, (lambda: share(0, 0), lambda: share(0, 1))), a_unit(0, 1),
            b_other(1, 0), b_other(1, 1), b_own(1, 0),
            b_own(1, 1, (lambda: second(w_group, z_group, 0, Z_SLOTS),)),
            a_unit(1, 0, (lambda: share(1, 0), lambda: share(1, 1))), a_unit(1, 1),
        ],
        (scores_even, scores_odd),
    )
    second(x_group, y_group, 0, Y_SLOTS)
    second(x_group, y_group, 1, Y_SLOTS)
    second(w_group, z_group, 1, Z_SLOTS)
    y_group.wait_recv()
    finish(y_group.parts(PART), (aa * 16 + ba) * PART, warped_one, flow_one)
    z_group.wait_recv()
    finish(z_group.parts(PART), (ba * 32 + aa) * PART, warped_two, flow_two)

    for u in range(4):
        core_copy[u].wait_send()
    for group in (x_group, w_group):
        group.wait_send(0)
        group.wait_send(1)
    y_group.wait_send()
    z_group.wait_send()


def emit(w1, g1, w2, g2, warped_one, flow_one, warped_two, flow_two, done):
    pairs = ((w1, warped_one), (g1, flow_one), (w2, warped_two), (g2, flow_two))
    copies = [pltpu.make_async_copy(src, dst, done.at[i]) for i, (src, dst) in enumerate(pairs)]
    for copy in copies:
        copy.start()
    for copy in copies:
        copy.wait()


def shards(frame_one, frame_two):
    rows_one, rows_two = frame_one.shape[0], frame_two.shape[0]
    vmem = pl.BlockSpec(memory_space=pltpu.VMEM)
    hbm = pl.BlockSpec(memory_space=pltpu.HBM)
    dma = pltpu.SemaphoreType.DMA
    shapes = (
        jax.ShapeDtypeStruct((PART, CH), F32),
        jax.ShapeDtypeStruct((2, PART), F32),
        jax.ShapeDtypeStruct((PART, CH), F32),
        jax.ShapeDtypeStruct((2, PART), F32),
    )
    results = pl.pallas_call(
        kernel,
        out_shape=shapes,
        in_specs=[hbm, hbm],
        out_specs=(vmem,) * 4,
        scratch_shapes=[
            pltpu.VMEM((rows_one, CH), BF16),
            pltpu.VMEM((rows_two, CH), BF16),
            pltpu.VMEM((AUG, rows_one), BF16),
            pltpu.VMEM((AUG, rows_two), BF16),
            pltpu.VMEM((rows_two, CHUNK), F32),
            pltpu.VMEM((rows_two, CHUNK), F32),
            pltpu.VMEM((4, MSG, CHUNK), F32),
            pltpu.VMEM((4, MSG, CHUNK), F32),
            pltpu.VMEM((4, MSG, CHUNK), F32),
            pltpu.VMEM((8, MSG, CH), F32),
            pltpu.VMEM((8, MSG, CH), F32),
            pltpu.VMEM((8, MSG, CH), F32),
            pltpu.VMEM((8, MSG, CH), F32),
            pltpu.VMEM((4, PACK, CH), F32),
            pltpu.VMEM((4, PACK, CH), F32),
            pltpu.VMEM((4, PACK, CH), F32),
            pltpu.VMEM((4, PACK, CH), F32),
            dma((2,)),
            dma((4,)), dma((4,)),
            dma((8,)), dma((8,)),
            dma((8,)), dma((8,)),
            dma((4,)), dma((4,)),
            dma((4,)), dma((4,)),
            pltpu.SemaphoreType.REGULAR((4,)),
            pltpu.SemaphoreType.REGULAR((4,)),
        ],
        compiler_params=pltpu.CompilerParams(
            collective_id=0, has_side_effects=True, vmem_limit_bytes=54976 * 1024
        ),
        name="match",
    )(frame_one, frame_two)
    return pl.pallas_call(
        emit,
        out_shape=shapes,
        in_specs=[vmem] * 4,
        out_specs=(hbm,) * 4,
        scratch_shapes=[dma((4,))],
        compiler_params=pltpu.CompilerParams(vmem_limit_bytes=1024 * 1024),
        name="emit",
    )(*results)


def solution(mesh):
    return jax.shard_map(
        shards,
        mesh=mesh,
        in_specs=(P("aa", None), P("ba", None)),
        out_specs=(
            P(("aa", "ba"), None),
            P(None, ("aa", "ba")),
            P(("ba", "aa"), None),
            P(None, ("ba", "aa")),
        ),
        check_vma=False,
    )
```

```python
import functools
import math

import jax
import jax.numpy as jnp
from jax import lax
from jax.experimental import pallas as pl
from jax.experimental.pallas import tpu as pltpu
from jax.sharding import PartitionSpec as P

IMG_W = 128
CH = 128
MSG = CH + 8
AUG = CH + 16
CHUNK = 256
PART = 64
PACK = PART + 8
TILE = 512
SCALE = CH ** (-0.5) * math.log2(math.e)
MESH = pl.DeviceIdType.MESH
Y_ORDER = (0, 1, 3, 2)
F32 = jnp.float32
BF16 = jnp.bfloat16


def grid_xy(pixel):
    column_pos = lax.rem(pixel, IMG_W).astype(F32) / 64.0
    row_pos = lax.div(pixel, IMG_W).astype(F32) / 64.0
    return column_pos, row_pos


def put_keys(kt, start, keys, first_pixel):
    count = keys.shape[0]
    cols = pl.ds(start, count)
    kt[0:CH, cols] = keys.T
    row = lax.broadcasted_iota(jnp.int32, (16, count), 0)
    pixel = first_pixel + lax.broadcasted_iota(jnp.int32, (16, count), 1)
    column_pos, row_pos = grid_xy(pixel)
    extra = jnp.where(row == 0, column_pos, jnp.where(row == 1, row_pos, jnp.where(row == 2, 1.0, 0.0)))
    kt[CH:AUG, cols] = extra.astype(BF16)


def score_steps(queries, keys, scores, peaks):
    def step(first):
        rows = slice(first, first + TILE)
        tile = lax.dot_general(
            keys[rows], queries, (((1,), (1,)), ((), ())), preferred_element_type=F32
        )
        scores[rows] = tile
        peaks.append(jnp.max(tile.reshape(TILE // 8, 8, CHUNK), axis=0))

    return [functools.partial(step, first) for first in range(0, keys.shape[0], TILE)]


def sum_steps(kt, scores, peak, sums):
    def step(first):
        cols = slice(first, first + TILE)
        weights = jnp.exp2((scores[cols] - peak) * SCALE).astype(BF16)
        sums.append(jnp.dot(kt[:, cols], weights, preferred_element_type=F32))

    return [functools.partial(step, first) for first in range(0, kt.shape[1], TILE)]


def attend(units, scores):
    peaks = []
    for step in score_steps(units[0][0](), units[0][1], scores[0], peaks):
        step()
    for i, (_, _, kt, use) in enumerate(units):
        peak = jnp.max(functools.reduce(jnp.maximum, peaks), axis=0, keepdims=True)
        sums, peaks = [], []
        ahead = []
        if i + 1 < len(units):
            ahead = score_steps(units[i + 1][0](), units[i + 1][1], scores[(i + 1) % 2], peaks)
        now = sum_steps(kt, scores[i % 2], peak, sums)
        for step in ahead + now:
            step()
        total = functools.reduce(jnp.add, sums)
        row = lax.broadcasted_iota(jnp.int32, (8, CHUNK), 0)
        use(total[0:CH], jnp.where(row == 3, peak, total[CH:MSG]))


def merge(parts):
    peaks = [extra[3:4] for _, extra in parts]
    peak = functools.reduce(jnp.maximum, peaks)
    gains = [jnp.exp2((p - peak) * SCALE) for p in peaks]
    feat = sum(f * g for (f, _), g in zip(parts, gains))
    extra = sum(e * g for (_, e), g in zip(parts, gains))
    row = lax.broadcasted_iota(jnp.int32, extra.shape, 0)
    return feat, jnp.where(row == 3, peak, extra)


def pack(feat, extra, out, first):
    low_lane = lax.broadcasted_iota(jnp.int32, (PART, CH), 1) < PART
    low_extra = lax.broadcasted_iota(jnp.int32, (8, CH), 1) < PART
    for t in range(2):
        lanes = slice(t * CH, (t + 1) * CH)
        low, high, ext = feat[0:PART, lanes], feat[PART:CH, lanes], extra[:, lanes]
        turned = pltpu.roll(ext, PART, 1)
        even, odd = first + 2 * t, first + 2 * t + 1
        out[even, 0:PART] = jnp.where(low_lane, low, pltpu.roll(high, PART, 1))
        out[even, PART:PACK] = jnp.where(low_extra, ext, turned)
        out[odd, 0:PART] = jnp.where(low_lane, pltpu.roll(low, PART, 1), high)
        out[odd, PART:PACK] = jnp.where(low_extra, turned, ext)


def finish(parts, first_pixel, warped, flow):
    feat, extra = merge(parts)
    inverse = 1.0 / extra[2:3]
    turned = (feat * inverse).T
    warped[:, 0:PART] = turned[0:PART]
    warped[:, PART:CH] = turned[PART:CH]
    pixel = first_pixel + lax.broadcasted_iota(jnp.int32, (1, PART), 1)
    column_pos, row_pos = grid_xy(pixel)
    coord = (extra * inverse)[:, 0:PART]
    flow[0:1] = coord[0:1] - column_pos
    flow[1:2] = coord[1:2] - row_pos


class Group:
    def __init__(self, rank, peer, out, got, sems):
        self.rank, self.peer, self.out, self.got = rank, peer, out, got
        self.send_sem, self.recv_sem = sems

    def others(self):
        return [lax.rem(self.rank + t, 4) for t in range(1, 4)]

    def greet(self, barrier):
        for k in self.others():
            pl.semaphore_signal(barrier, inc=1, device_id=self.peer(k), device_id_type=MESH)

    def copy(self, k, e=0):
        to, mine = 4 * e + k, 4 * e + self.rank
        return pltpu.make_async_remote_copy(
            src_ref=self.out.at[to], dst_ref=self.got.at[mine],
            send_sem=self.send_sem.at[to], recv_sem=self.recv_sem.at[mine],
            device_id=self.peer(k), device_id_type=MESH,
        )

    def send(self, e):
        for k in self.others():
            self.copy(k, e).start()

    def wait_recv(self, e=0):
        for k in self.others():
            slot = 4 * e + k
            pltpu.make_async_remote_copy(
                src_ref=self.out.at[slot], dst_ref=self.got.at[slot],
                send_sem=self.send_sem.at[slot], recv_sem=self.recv_sem.at[slot],
                device_id=self.peer(k), device_id_type=MESH,
            ).wait_recv()

    def wait_send(self, e=0):
        for k in self.others():
            self.copy(k, e).wait_send()

    def parts(self, e=0):
        blocks = [self.out.at[4 * e + self.rank]] + [self.got.at[4 * e + k] for k in self.others()]
        return [(block[0:PART], block[PART:PACK]) for block in blocks]


class RankedGroup(Group):
    def __init__(self, rank, peer, out, got, sems):
        super().__init__(rank, peer, out, got, sems[0:2])
        self.ready = sems[2]

    def greet(self, barrier):
        for k in range(4):
            @pl.when(k > self.rank)
            def _():
                pl.semaphore_signal(barrier, inc=1, device_id=self.peer(k), device_id_type=MESH)

    def answer(self):
        for k in range(4):
            @pl.when(k < self.rank)
            def _():
                pl.semaphore_signal(
                    self.ready.at[self.rank], inc=1, device_id=self.peer(k), device_id_type=MESH
                )

    def send_lower(self, k):
        @pl.when(k < self.rank)
        def _():
            self.copy(k).start()

    def send_higher(self, k):
        @pl.when(k > self.rank)
        def _():
            pl.semaphore_wait(self.ready.at[k], 1)
            self.copy(k).start()


def kernel(
    f1_hbm, f2_hbm, warped_one, flow_one, warped_two, flow_two,
    f1, f2, kt_one, kt_two, scores_even, scores_odd,
    core_out, core_in, core_own, x_out, x_in, w_out, w_in, y_out, y_in, z_out, z_in,
    load, core_send, core_recv, x_send, x_recv, w_send, w_recv, y_send, y_recv, z_send, z_recv,
    y_ready, z_ready,
):
    load_one = pltpu.make_async_copy(f1_hbm, f1, load.at[0])
    load_two = pltpu.make_async_copy(f2_hbm, f2, load.at[1])
    load_one.start()
    load_two.start()

    aa, ba = lax.axis_index("aa"), lax.axis_index("ba")
    core = lax.rem(aa, 2)
    z = lax.rem(lax.div(aa, 2), 8)
    y_lo = lax.div(aa, 16)
    z_hi, z_lo = lax.div(z, 2), lax.rem(z, 2)
    x, y_hi = lax.div(ba, 4), lax.rem(ba, 4)

    def y_slot(value):
        return value + lax.div(value, 2) * (5 - 2 * value)

    sibling = (aa + 1 - 2 * core, ba)
    x_group = Group(x, lambda k: (aa, k * 4 + y_hi), x_out, x_in, (x_send, x_recv))
    w_group = Group(
        y_lo * 2 + z_lo,
        lambda k: ((lax.div(k, 2) * 8 + z_hi * 2 + lax.rem(k, 2)) * 2 + core, ba),
        w_out, w_in, (w_send, w_recv),
    )
    y_group = RankedGroup(
        y_slot(y_hi), lambda k: (aa, x * 4 + y_slot(k)), y_out, y_in, (y_send, y_recv, y_ready)
    )
    z_group = RankedGroup(
        z_hi, lambda k: ((y_lo * 8 + k * 2 + z_lo) * 2 + core, ba), z_out, z_in, (z_send, z_recv, z_ready)
    )

    barrier = pltpu.get_barrier_semaphore()
    pl.semaphore_signal(barrier, inc=1, device_id=sibling, device_id_type=MESH)
    for group in (w_group, x_group, z_group, y_group):
        group.greet(barrier)

    load_one.wait()
    put_keys(kt_one, 0, f1[...], aa * f1.shape[0])
    load_two.wait()

    core_copy = [
        pltpu.make_async_remote_copy(
            src_ref=core_out.at[u], dst_ref=core_in.at[u],
            send_sem=core_send.at[u], recv_sem=core_recv.at[u],
            device_id=sibling, device_id_type=MESH,
        )
        for u in range(4)
    ]

    def b_queries(e, parity):
        blocks = []
        for k in range(4):
            block = (k // 2) * 8 + 2 * e + k % 2
            start = pl.multiple_of((block * 2 + parity) * PART, PART)
            blocks.append(f2[pl.ds(start, PART)])
        return jnp.concatenate(blocks, axis=0)

    def a_queries(e):
        starts = [k * CHUNK + Y_ORDER[e] * PART for k in range(4)]
        return jnp.concatenate([f1[start:start + PART] for start in starts], axis=0)

    def put(out, feat, extra):
        out[0:CH] = feat
        out[CH:MSG] = extra

    def enter():
        pl.semaphore_wait(barrier, 7 + y_group.rank + z_group.rank)
        core_copy[0].start()
        z_group.answer()
        y_group.answer()

    def share(e):
        core_copy[e].wait_recv()
        mine, got = core_own.at[e], core_in.at[e]
        feat, extra = merge([(mine[0:CH], mine[CH:MSG]), (got[0:CH], got[CH:MSG])])
        pack(feat, extra, w_out, 4 * e)
        w_group.send(e)

    def second(first_group, second_group, e):
        first_group.wait_recv(e)
        feat, extra = merge(first_group.parts(e))
        second_group.out[e, 0:PART] = feat
        second_group.out[e, PART:PACK] = extra
        second_group.send_lower(e)

    def b_other(e, *after):
        def use(feat, extra):
            put(core_out.at[e], feat, extra)
            if e:
                core_copy[e].start()
            for step in after:
                step()

        return functools.partial(b_queries, e, 1 - core), f1, kt_one, use

    def b_own(e, *after):
        def use(feat, extra):
            put(core_own.at[e], feat, extra)
            for step in after:
                step()

        return functools.partial(b_queries, e, core), f1, kt_one, use

    def a_unit(e, *after):
        def use(feat, extra):
            pack(feat, extra, x_out, 4 * e)
            x_group.send(e)
            for step in after:
                step()

        return functools.partial(a_queries, e), f2, kt_two, use

    def late_keys():
        put_keys(kt_two, 0, f2[...], ba * f2.shape[0])

    def do(step, *args):
        return functools.partial(step, *args)

    attend(
        [
            b_other(0), b_own(0, enter, late_keys), b_other(1), b_own(1), b_other(2, do(share, 0)),
            a_unit(0, do(share, 1)), b_own(2), a_unit(1), b_other(3), b_own(3),
            a_unit(2, do(second, w_group, z_group, 0), do(share, 2), do(share, 3)),
            a_unit(3, do(second, w_group, z_group, 1)),
        ],
        (scores_even, scores_odd),
    )
    second(x_group, y_group, 0)
    second(x_group, y_group, 1)
    for k in range(2):
        y_group.send_higher(k)
    second(w_group, z_group, 2)
    second(x_group, y_group, 2)
    second(w_group, z_group, 3)
    second(x_group, y_group, 3)
    for k in range(2, 4):
        y_group.send_higher(k)
    for k in range(4):
        z_group.send_higher(k)
    y_group.wait_recv()
    finish(y_group.parts(), (aa * 16 + ba) * PART, warped_one, flow_one)
    for e in range(4):
        core_copy[e].wait_send()
        x_group.wait_send(e)
        w_group.wait_send(e)
    y_group.wait_send()
    z_group.wait_send()
    z_group.wait_recv()
    finish(z_group.parts(), (ba * 32 + aa) * PART, warped_two, flow_two)


def emit(w1, g1, w2, g2, warped_one, flow_one, warped_two, flow_two, done):
    pairs = ((w1, warped_one), (g1, flow_one), (w2, warped_two), (g2, flow_two))
    copies = [pltpu.make_async_copy(src, dst, done.at[i]) for i, (src, dst) in enumerate(pairs)]
    for copy in copies:
        copy.start()
    for copy in copies:
        copy.wait()


def shards(frame_one, frame_two):
    rows_one, rows_two = frame_one.shape[0], frame_two.shape[0]
    vmem = pl.BlockSpec(memory_space=pltpu.VMEM)
    hbm = pl.BlockSpec(memory_space=pltpu.HBM)
    dma = pltpu.SemaphoreType.DMA
    shapes = (
        jax.ShapeDtypeStruct((PART, CH), F32),
        jax.ShapeDtypeStruct((2, PART), F32),
        jax.ShapeDtypeStruct((PART, CH), F32),
        jax.ShapeDtypeStruct((2, PART), F32),
    )
    results = pl.pallas_call(
        kernel,
        out_shape=shapes,
        in_specs=[hbm, hbm],
        out_specs=(vmem,) * 4,
        scratch_shapes=[
            pltpu.VMEM((rows_one, CH), BF16),
            pltpu.VMEM((rows_two, CH), BF16),
            pltpu.VMEM((AUG, rows_one), BF16),
            pltpu.VMEM((AUG, rows_two), BF16),
            pltpu.VMEM((rows_two, CHUNK), F32),
            pltpu.VMEM((rows_two, CHUNK), F32),
            pltpu.VMEM((4, MSG, CHUNK), F32),
            pltpu.VMEM((4, MSG, CHUNK), F32),
            pltpu.VMEM((4, MSG, CHUNK), F32),
            pltpu.VMEM((16, PACK, CH), F32),
            pltpu.VMEM((16, PACK, CH), F32),
            pltpu.VMEM((16, PACK, CH), F32),
            pltpu.VMEM((16, PACK, CH), F32),
            pltpu.VMEM((4, PACK, CH), F32),
            pltpu.VMEM((4, PACK, CH), F32),
            pltpu.VMEM((4, PACK, CH), F32),
            pltpu.VMEM((4, PACK, CH), F32),
            dma((2,)),
            dma((4,)), dma((4,)),
            dma((16,)), dma((16,)),
            dma((16,)), dma((16,)),
            dma((4,)), dma((4,)),
            dma((4,)), dma((4,)),
            pltpu.SemaphoreType.REGULAR((4,)),
            pltpu.SemaphoreType.REGULAR((4,)),
        ],
        compiler_params=pltpu.CompilerParams(
            collective_id=0, has_side_effects=True, vmem_limit_bytes=54976 * 1024
        ),
        name="match",
    )(frame_one, frame_two)
    return pl.pallas_call(
        emit,
        out_shape=shapes,
        in_specs=[vmem] * 4,
        out_specs=(hbm,) * 4,
        scratch_shapes=[dma((4,))],
        compiler_params=pltpu.CompilerParams(vmem_limit_bytes=1024 * 1024),
        name="emit",
    )(*results)


def solution(mesh):
    return jax.shard_map(
        shards,
        mesh=mesh,
        in_specs=(P("aa", None), P("ba", None)),
        out_specs=(
            P(("aa", "ba"), None),
            P(None, ("aa", "ba")),
            P(("ba", "aa"), None),
            P(None, ("ba", "aa")),
        ),
        check_vma=False,
    )
```

```python
import functools
import math

import jax
import jax.numpy as jnp
from jax import lax
from jax.experimental import pallas as pl
from jax.experimental.pallas import tpu as pltpu
from jax.sharding import PartitionSpec as P

IMG_W = 128
CH = 128
EXTRA = 4
MSG = CH + EXTRA
AUG = CH + 16
CHUNK = 256
PART = 64
PACK = PART + EXTRA
TILE = 512
SCALE = CH ** (-0.5) * math.log2(math.e)
MESH = pl.DeviceIdType.MESH
Y_ORDER = (0, 1, 3, 2)
F32 = jnp.float32
BF16 = jnp.bfloat16


def grid_xy(pixel):
    column_pos = lax.rem(pixel, IMG_W).astype(F32) / 64.0
    row_pos = lax.div(pixel, IMG_W).astype(F32) / 64.0
    return column_pos, row_pos


def put_keys(kt, start, keys, first_pixel):
    count = keys.shape[0]
    cols = pl.ds(start, count)
    kt[0:CH, cols] = keys.T
    row = lax.broadcasted_iota(jnp.int32, (16, count), 0)
    pixel = first_pixel + lax.broadcasted_iota(jnp.int32, (16, count), 1)
    column_pos, row_pos = grid_xy(pixel)
    extra = jnp.where(row == 0, column_pos, jnp.where(row == 1, row_pos, jnp.where(row == 2, 1.0, 0.0)))
    kt[CH:AUG, cols] = extra.astype(BF16)


def score_steps(queries, keys, scores, peaks):
    def step(first):
        rows = slice(first, first + TILE)
        tile = lax.dot_general(
            keys[rows], queries, (((1,), (1,)), ((), ())), preferred_element_type=F32
        )
        scores[rows] = tile
        peaks.append(jnp.max(tile.reshape(TILE // 8, 8, CHUNK), axis=0))

    return [functools.partial(step, first) for first in range(0, keys.shape[0], TILE)]


def sum_steps(kt, scores, peak, sums):
    def step(first):
        cols = slice(first, first + TILE)
        weights = jnp.exp2((scores[cols] - peak) * SCALE).astype(BF16)
        sums.append(jnp.dot(kt[:, cols], weights, preferred_element_type=F32))

    return [functools.partial(step, first) for first in range(0, kt.shape[1], TILE)]


def attend(units, scores):
    peaks = []
    for step in score_steps(units[0][0](), units[0][1], scores[0], peaks):
        step()
    for i, (_, _, kt, use) in enumerate(units):
        peak = jnp.max(functools.reduce(jnp.maximum, peaks), axis=0, keepdims=True)
        sums, peaks = [], []
        ahead = []
        if i + 1 < len(units):
            ahead = score_steps(units[i + 1][0](), units[i + 1][1], scores[(i + 1) % 2], peaks)
        now = sum_steps(kt, scores[i % 2], peak, sums)
        for step in ahead + now:
            step()
        total = functools.reduce(jnp.add, sums)
        row = lax.broadcasted_iota(jnp.int32, (EXTRA, CHUNK), 0)
        use(total[0:CH], jnp.where(row == 3, peak, total[CH:MSG]))


def merge(parts):
    peaks = [extra[3:4] for _, extra in parts]
    peak = functools.reduce(jnp.maximum, peaks)
    gains = [jnp.exp2((p - peak) * SCALE) for p in peaks]
    feat = sum(f * g for (f, _), g in zip(parts, gains))
    extra = sum(e * g for (_, e), g in zip(parts, gains))
    row = lax.broadcasted_iota(jnp.int32, extra.shape, 0)
    return feat, jnp.where(row == 3, peak, extra)


def pack(feat, extra, out, first):
    low_lane = lax.broadcasted_iota(jnp.int32, (PART, CH), 1) < PART
    low_extra = lax.broadcasted_iota(jnp.int32, (EXTRA, CH), 1) < PART
    for t in range(2):
        lanes = slice(t * CH, (t + 1) * CH)
        low, high, ext = feat[0:PART, lanes], feat[PART:CH, lanes], extra[:, lanes]
        turned = pltpu.roll(ext, PART, 1)
        even, odd = first + 2 * t, first + 2 * t + 1
        out[even, 0:PART] = jnp.where(low_lane, low, pltpu.roll(high, PART, 1))
        out[even, PART:PACK] = jnp.where(low_extra, ext, turned)
        out[odd, 0:PART] = jnp.where(low_lane, pltpu.roll(low, PART, 1), high)
        out[odd, PART:PACK] = jnp.where(low_extra, turned, ext)


def finish(parts, first_pixel, warped, flow):
    feat, extra = merge(parts)
    inverse = 1.0 / extra[2:3]
    turned = (feat * inverse).T
    warped[:, 0:PART] = turned[0:PART]
    warped[:, PART:CH] = turned[PART:CH]
    pixel = first_pixel + lax.broadcasted_iota(jnp.int32, (1, PART), 1)
    column_pos, row_pos = grid_xy(pixel)
    coord = (extra * inverse)[:, 0:PART]
    flow[0:1] = coord[0:1] - column_pos
    flow[1:2] = coord[1:2] - row_pos


class Group:
    def __init__(self, rank, peer, out, got, sems, span=1):
        self.rank, self.peer, self.out, self.got, self.span = rank, peer, out, got, span
        self.send_sem, self.recv_sem, self.ready = sems
        self.level = lax.div(rank, span)
        self.greeted = self.level * span + span - 1

    def others(self):
        return [lax.rem(self.rank + t, 4) for t in range(1, 4)]

    def greet(self, barrier):
        for k in range(4):
            @pl.when((k // self.span >= self.level) & (k != self.rank))
            def _():
                pl.semaphore_signal(barrier, inc=1, device_id=self.peer(k), device_id_type=MESH)

    def answer(self):
        for k in range(4 - self.span):
            @pl.when(k // self.span < self.level)
            def _():
                pl.semaphore_signal(
                    self.ready.at[self.rank], inc=1, device_id=self.peer(k), device_id_type=MESH
                )

    def wait_ready(self, k):
        pl.semaphore_wait(self.ready.at[k], 1)

    def copy(self, k, e=0):
        to, mine = 4 * e + k, 4 * e + self.rank
        return pltpu.make_async_remote_copy(
            src_ref=self.out.at[to], dst_ref=self.got.at[mine],
            send_sem=self.send_sem.at[to], recv_sem=self.recv_sem.at[mine],
            device_id=self.peer(k), device_id_type=MESH,
        )

    def send_lower(self, k, e=0):
        @pl.when((k // self.span <= self.level) & (k != self.rank))
        def _():
            self.copy(k, e).start()

    def send_higher(self, k, e=0):
        @pl.when(k // self.span > self.level)
        def _():
            self.wait_ready(k)
            self.copy(k, e).start()

    def send(self, e):
        if e == 0:
            for k in range(4):
                self.send_lower(k)
        else:
            for k in self.others():
                self.copy(k, e).start()

    def send_first(self):
        for k in range(self.span, 4):
            self.send_higher(k)

    def wait_recv(self, e=0):
        for k in self.others():
            slot = 4 * e + k
            pltpu.make_async_remote_copy(
                src_ref=self.out.at[slot], dst_ref=self.got.at[slot],
                send_sem=self.send_sem.at[slot], recv_sem=self.recv_sem.at[slot],
                device_id=self.peer(k), device_id_type=MESH,
            ).wait_recv()

    def wait_send(self, e=0):
        for k in self.others():
            self.copy(k, e).wait_send()

    def parts(self, e=0):
        blocks = [self.out.at[4 * e + self.rank]] + [self.got.at[4 * e + k] for k in self.others()]
        return [(block[0:PART], block[PART:PACK]) for block in blocks]


def kernel(
    f1_hbm, f2_hbm, warped_one, flow_one, warped_two, flow_two,
    f1, f2, kt_one, kt_two, scores_even, scores_odd,
    core_out, core_in, core_own, x_out, x_in, w_out, w_in, y_out, y_in, z_out, z_in,
    load, core_send, core_recv, x_send, x_recv, w_send, w_recv, y_send, y_recv, z_send, z_recv,
    x_ready, w_ready, y_ready, z_ready,
):
    load_one = pltpu.make_async_copy(f1_hbm, f1, load.at[0])
    load_two = pltpu.make_async_copy(f2_hbm, f2, load.at[1])
    load_one.start()
    load_two.start()

    aa, ba = lax.axis_index("aa"), lax.axis_index("ba")
    core = lax.rem(aa, 2)
    z = lax.rem(lax.div(aa, 2), 8)
    y_lo = lax.div(aa, 16)
    z_hi, z_lo = lax.div(z, 2), lax.rem(z, 2)
    x, y_hi = lax.div(ba, 4), lax.rem(ba, 4)

    def y_slot(value):
        return value + lax.div(value, 2) * (5 - 2 * value)

    sibling = (aa + 1 - 2 * core, ba)
    def w_peer(k):
        return ((lax.rem(k, 2) * 8 + z_hi * 2 + lax.div(k, 2)) * 2 + core, ba)

    x_group = Group(x, lambda k: (aa, k * 4 + y_hi), x_out, x_in, (x_send, x_recv, x_ready))
    w_group = Group(
        z_lo * 2 + y_lo, w_peer, w_out, w_in, (w_send, w_recv, w_ready), 4
    )
    y_group = Group(
        y_slot(y_hi), lambda k: (aa, x * 4 + y_slot(k)), y_out, y_in, (y_send, y_recv, y_ready)
    )
    z_group = Group(
        z_hi, lambda k: ((y_lo * 8 + k * 2 + z_lo) * 2 + core, ba), z_out, z_in, (z_send, z_recv, z_ready)
    )

    barrier = pltpu.get_barrier_semaphore()
    pl.semaphore_signal(barrier, inc=1, device_id=sibling, device_id_type=MESH)
    groups = (w_group, x_group, z_group, y_group)
    for group in groups:
        group.greet(barrier)

    load_one.wait()
    put_keys(kt_one, 0, f1[...], aa * f1.shape[0])
    load_two.wait()

    core_copy = [
        pltpu.make_async_remote_copy(
            src_ref=core_out.at[u], dst_ref=core_in.at[u],
            send_sem=core_send.at[u], recv_sem=core_recv.at[u],
            device_id=sibling, device_id_type=MESH,
        )
        for u in range(4)
    ]

    def b_queries(e, parity):
        blocks = []
        for k in range(4):
            block = (k % 2) * 8 + 2 * e + k // 2
            start = pl.multiple_of((block * 2 + parity) * PART, PART)
            blocks.append(f2[pl.ds(start, PART)])
        return jnp.concatenate(blocks, axis=0)

    def a_queries(e):
        starts = [k * CHUNK + Y_ORDER[e] * PART for k in range(4)]
        return jnp.concatenate([f1[start:start + PART] for start in starts], axis=0)

    def put(out, feat, extra):
        out[0:CH] = feat
        out[CH:MSG] = extra

    def enter():
        pl.semaphore_wait(barrier, 1 + sum(group.greeted for group in groups))
        core_copy[0].start()
        for group in groups:
            group.answer()

    def share(e):
        core_copy[e].wait_recv()
        mine, got = core_own.at[e], core_in.at[e]
        feat, extra = merge([(mine[0:CH], mine[CH:MSG]), (got[0:CH], got[CH:MSG])])
        pack(feat, extra, w_out, 4 * e)
        w_group.send(e)

    def second(first_group, second_group, e):
        first_group.wait_recv(e)
        feat, extra = merge(first_group.parts(e))
        second_group.out[e, 0:PART] = feat
        second_group.out[e, PART:PACK] = extra
        second_group.send_lower(e)

    def b_other(e, *after):
        def use(feat, extra):
            put(core_out.at[e], feat, extra)
            if e:
                core_copy[e].start()
            for step in after:
                step()

        return functools.partial(b_queries, e, 1 - core), f1, kt_one, use

    def b_own(e, *after):
        def use(feat, extra):
            put(core_own.at[e], feat, extra)
            for step in after:
                step()

        return functools.partial(b_queries, e, core), f1, kt_one, use

    def a_unit(e, *after):
        def use(feat, extra):
            pack(feat, extra, x_out, 4 * e)
            if e != 1:
                x_group.send(e)
            for step in after:
                step()

        return functools.partial(a_queries, e), f2, kt_two, use

    def late_keys():
        put_keys(kt_two, 0, f2[...], ba * f2.shape[0])

    def do(step, *args):
        return functools.partial(step, *args)

    attend(
        [
            b_other(0, enter), b_own(0, late_keys), b_other(1), b_own(1), b_other(2, do(share, 0)),
            a_unit(0, do(share, 1)), b_own(2), a_unit(1), b_other(3),
            b_own(3, x_group.send_first, do(x_group.send, 1)),
            a_unit(2, do(second, w_group, z_group, 0), do(share, 2)),
            a_unit(3, do(second, w_group, z_group, 1), do(share, 3)),
        ],
        (scores_even, scores_odd),
    )
    second(x_group, y_group, 0)
    second(x_group, y_group, 1)
    for k in range(2):
        y_group.send_higher(k)
    second(x_group, y_group, 2)
    second(x_group, y_group, 3)
    for k in range(2, 4):
        y_group.send_higher(k)
    second(w_group, z_group, 2)
    second(w_group, z_group, 3)
    for k in range(4):
        z_group.send_higher(k)
    y_group.wait_recv()
    finish(y_group.parts(), (aa * 16 + ba) * PART, warped_one, flow_one)
    for e in range(4):
        core_copy[e].wait_send()
        x_group.wait_send(e)
        w_group.wait_send(e)
    z_group.wait_recv()
    finish(z_group.parts(), (ba * 32 + aa) * PART, warped_two, flow_two)
    y_group.wait_send()
    z_group.wait_send()


def emit(w1, g1, w2, g2, warped_one, flow_one, warped_two, flow_two, done):
    pairs = ((w1, warped_one), (g1, flow_one), (w2, warped_two), (g2, flow_two))
    copies = [pltpu.make_async_copy(src, dst, done.at[i]) for i, (src, dst) in enumerate(pairs)]
    for copy in copies:
        copy.start()
    for copy in copies:
        copy.wait()


def shards(frame_one, frame_two):
    rows_one, rows_two = frame_one.shape[0], frame_two.shape[0]
    vmem = pl.BlockSpec(memory_space=pltpu.VMEM)
    hbm = pl.BlockSpec(memory_space=pltpu.HBM)
    dma = pltpu.SemaphoreType.DMA
    shapes = (
        jax.ShapeDtypeStruct((PART, CH), F32),
        jax.ShapeDtypeStruct((2, PART), F32),
        jax.ShapeDtypeStruct((PART, CH), F32),
        jax.ShapeDtypeStruct((2, PART), F32),
    )
    results = pl.pallas_call(
        kernel,
        out_shape=shapes,
        in_specs=[hbm, hbm],
        out_specs=(vmem,) * 4,
        scratch_shapes=[
            pltpu.VMEM((rows_one, CH), BF16),
            pltpu.VMEM((rows_two, CH), BF16),
            pltpu.VMEM((AUG, rows_one), BF16),
            pltpu.VMEM((AUG, rows_two), BF16),
            pltpu.VMEM((rows_two, CHUNK), F32),
            pltpu.VMEM((rows_two, CHUNK), F32),
            pltpu.VMEM((4, MSG, CHUNK), F32),
            pltpu.VMEM((4, MSG, CHUNK), F32),
            pltpu.VMEM((4, MSG, CHUNK), F32),
            pltpu.VMEM((16, PACK, CH), F32),
            pltpu.VMEM((16, PACK, CH), F32),
            pltpu.VMEM((16, PACK, CH), F32),
            pltpu.VMEM((16, PACK, CH), F32),
            pltpu.VMEM((4, PACK, CH), F32),
            pltpu.VMEM((4, PACK, CH), F32),
            pltpu.VMEM((4, PACK, CH), F32),
            pltpu.VMEM((4, PACK, CH), F32),
            dma((2,)),
            dma((4,)), dma((4,)),
            dma((16,)), dma((16,)),
            dma((16,)), dma((16,)),
            dma((4,)), dma((4,)),
            dma((4,)), dma((4,)),
            pltpu.SemaphoreType.REGULAR((4,)),
            pltpu.SemaphoreType.REGULAR((4,)),
            pltpu.SemaphoreType.REGULAR((4,)),
            pltpu.SemaphoreType.REGULAR((4,)),
        ],
        compiler_params=pltpu.CompilerParams(
            collective_id=0, has_side_effects=True, vmem_limit_bytes=54976 * 1024
        ),
        name="match",
    )(frame_one, frame_two)
    return pl.pallas_call(
        emit,
        out_shape=shapes,
        in_specs=[vmem] * 4,
        out_specs=(hbm,) * 4,
        scratch_shapes=[dma((4,))],
        compiler_params=pltpu.CompilerParams(vmem_limit_bytes=1024 * 1024),
        name="emit",
    )(*results)


def solution(mesh):
    return jax.shard_map(
        shards,
        mesh=mesh,
        in_specs=(P("aa", None), P("ba", None)),
        out_specs=(
            P(("aa", "ba"), None),
            P(None, ("aa", "ba")),
            P(("ba", "aa"), None),
            P(None, ("ba", "aa")),
        ),
        check_vma=False,
    )
```

```python
import functools
import math

import jax
import jax.numpy as jnp
from jax import lax
from jax.experimental import pallas as pl
from jax.experimental.pallas import tpu as pltpu
from jax.sharding import PartitionSpec as P

IMG_W = 128
CH = 128
EXTRA = 4
MSG = CH + EXTRA
AUG = CH + 16
CHUNK = 256
PART = 64
PACK = PART + EXTRA
TILE = 512
SCALE = CH ** (-0.5) * math.log2(math.e)
MESH = pl.DeviceIdType.MESH
Y_ORDER = (0, 1, 3, 2)
F32 = jnp.float32
BF16 = jnp.bfloat16


def grid_xy(pixel):
    column_pos = lax.rem(pixel, IMG_W).astype(F32) / 64.0
    row_pos = lax.div(pixel, IMG_W).astype(F32) / 64.0
    return column_pos, row_pos


def put_keys(kt, start, keys, first_pixel):
    count = keys.shape[0]
    cols = pl.ds(start, count)
    kt[0:CH, cols] = keys.T
    row = lax.broadcasted_iota(jnp.int32, (16, count), 0)
    pixel = first_pixel + lax.broadcasted_iota(jnp.int32, (16, count), 1)
    column_pos, row_pos = grid_xy(pixel)
    extra = jnp.where(row == 0, column_pos, jnp.where(row == 1, row_pos, jnp.where(row == 2, 1.0, 0.0)))
    kt[CH:AUG, cols] = extra.astype(BF16)


def score_steps(queries, keys, scores, peaks):
    def step(first):
        rows = slice(first, first + TILE)
        tile = lax.dot_general(
            keys[rows], queries, (((1,), (1,)), ((), ())), preferred_element_type=F32
        )
        scores[rows] = tile
        peaks.append(jnp.max(tile.reshape(TILE // 8, 8, CHUNK), axis=0))

    return [functools.partial(step, first) for first in range(0, keys.shape[0], TILE)]


def sum_steps(kt, scores, peak, sums):
    def step(first):
        cols = slice(first, first + TILE)
        weights = jnp.exp2((scores[cols] - peak) * SCALE).astype(BF16)
        sums.append(jnp.dot(kt[:, cols], weights, preferred_element_type=F32))

    return [functools.partial(step, first) for first in range(0, kt.shape[1], TILE)]


def attend(units, scores):
    peaks = []
    for step in score_steps(units[0][0](), units[0][1], scores[0], peaks):
        step()
    for i, (_, _, kt, use) in enumerate(units):
        peak = jnp.max(functools.reduce(jnp.maximum, peaks), axis=0, keepdims=True)
        sums, peaks = [], []
        ahead = []
        if i + 1 < len(units):
            ahead = score_steps(units[i + 1][0](), units[i + 1][1], scores[(i + 1) % 2], peaks)
        now = sum_steps(kt, scores[i % 2], peak, sums)
        for step in ahead + now:
            step()
        total = functools.reduce(jnp.add, sums)
        row = lax.broadcasted_iota(jnp.int32, (EXTRA, CHUNK), 0)
        use(total[0:CH], jnp.where(row == 3, peak, total[CH:MSG]))


def merge(parts):
    peaks = [extra[3:4] for _, extra in parts]
    peak = functools.reduce(jnp.maximum, peaks)
    gains = [jnp.exp2((p - peak) * SCALE) for p in peaks]
    feat = sum(f * g for (f, _), g in zip(parts, gains))
    extra = sum(e * g for (_, e), g in zip(parts, gains))
    row = lax.broadcasted_iota(jnp.int32, extra.shape, 0)
    return feat, jnp.where(row == 3, peak, extra)


def pack(feat, extra, out, first):
    low_lane = lax.broadcasted_iota(jnp.int32, (PART, CH), 1) < PART
    low_extra = lax.broadcasted_iota(jnp.int32, (EXTRA, CH), 1) < PART
    for t in range(2):
        lanes = slice(t * CH, (t + 1) * CH)
        low, high, ext = feat[0:PART, lanes], feat[PART:CH, lanes], extra[:, lanes]
        turned = pltpu.roll(ext, PART, 1)
        even, odd = first + 2 * t, first + 2 * t + 1
        out[even, 0:PART] = jnp.where(low_lane, low, pltpu.roll(high, PART, 1))
        out[even, PART:PACK] = jnp.where(low_extra, ext, turned)
        out[odd, 0:PART] = jnp.where(low_lane, pltpu.roll(low, PART, 1), high)
        out[odd, PART:PACK] = jnp.where(low_extra, turned, ext)


def finish(parts, first_pixel, warped, flow):
    feat, extra = merge(parts)
    inverse = 1.0 / extra[2:3]
    turned = (feat * inverse).T
    warped[:, 0:PART] = turned[0:PART]
    warped[:, PART:CH] = turned[PART:CH]
    pixel = first_pixel + lax.broadcasted_iota(jnp.int32, (1, PART), 1)
    column_pos, row_pos = grid_xy(pixel)
    coord = (extra * inverse)[:, 0:PART]
    flow[0:1] = coord[0:1] - column_pos
    flow[1:2] = coord[1:2] - row_pos


class Group:
    def __init__(self, rank, peer, out, got, sems, span=1):
        self.rank, self.peer, self.out, self.got, self.span = rank, peer, out, got, span
        self.send_sem, self.recv_sem, self.ready = sems
        self.level = lax.div(rank, span)
        self.greeted = self.level * span + span - 1

    def others(self):
        return [lax.rem(self.rank + t, 4) for t in range(1, 4)]

    def greet(self, barrier):
        for k in range(4):
            @pl.when((k // self.span >= self.level) & (k != self.rank))
            def _():
                pl.semaphore_signal(barrier, inc=1, device_id=self.peer(k), device_id_type=MESH)

    def answer(self):
        for k in range(4 - self.span):
            @pl.when(k // self.span < self.level)
            def _():
                pl.semaphore_signal(
                    self.ready.at[self.rank], inc=1, device_id=self.peer(k), device_id_type=MESH
                )

    def wait_ready(self, k):
        pl.semaphore_wait(self.ready.at[k], 1)

    def copy(self, k, e=0):
        to, mine = 4 * e + k, 4 * e + self.rank
        return pltpu.make_async_remote_copy(
            src_ref=self.out.at[to], dst_ref=self.got.at[mine],
            send_sem=self.send_sem.at[to], recv_sem=self.recv_sem.at[mine],
            device_id=self.peer(k), device_id_type=MESH,
        )

    def send_lower(self, k, e=0):
        @pl.when((k // self.span <= self.level) & (k != self.rank))
        def _():
            self.copy(k, e).start()

    def send_higher(self, k, e=0):
        @pl.when(k // self.span > self.level)
        def _():
            self.wait_ready(k)
            self.copy(k, e).start()

    def send(self, e):
        if e == 0:
            for k in range(4):
                self.send_lower(k)
        else:
            for k in self.others():
                self.copy(k, e).start()

    def send_first(self):
        for k in range(self.span, 4):
            self.send_higher(k)

    def wait_recv(self, e=0):
        for k in self.others():
            slot = 4 * e + k
            pltpu.make_async_remote_copy(
                src_ref=self.out.at[slot], dst_ref=self.got.at[slot],
                send_sem=self.send_sem.at[slot], recv_sem=self.recv_sem.at[slot],
                device_id=self.peer(k), device_id_type=MESH,
            ).wait_recv()

    def wait_send(self, e=0):
        for k in self.others():
            self.copy(k, e).wait_send()

    def parts(self, e=0):
        blocks = [self.out.at[4 * e + self.rank]] + [self.got.at[4 * e + k] for k in self.others()]
        return [(block[0:PART], block[PART:PACK]) for block in blocks]


def kernel(
    f1_hbm, f2_hbm, warped_one, flow_one, warped_two, flow_two,
    f1, f2, kt_one, kt_two, scores_even, scores_odd,
    core_out, core_in, core_own, x_out, x_in, w_out, w_in, y_out, y_in, z_out, z_in,
    load, core_send, core_recv, x_send, x_recv, w_send, w_recv, y_send, y_recv, z_send, z_recv,
    x_ready, w_ready, y_ready, z_ready,
):
    load_one = pltpu.make_async_copy(f1_hbm, f1, load.at[0])
    load_two = pltpu.make_async_copy(f2_hbm, f2, load.at[1])
    load_one.start()
    load_two.start()

    aa, ba = lax.axis_index("aa"), lax.axis_index("ba")
    core = lax.rem(aa, 2)
    z = lax.rem(lax.div(aa, 2), 8)
    y_lo = lax.div(aa, 16)
    z_hi, z_lo = lax.div(z, 2), lax.rem(z, 2)
    x, y_hi = lax.div(ba, 4), lax.rem(ba, 4)

    def y_slot(value):
        return value + lax.div(value, 2) * (5 - 2 * value)

    sibling = (aa + 1 - 2 * core, ba)
    def w_peer(k):
        return ((lax.rem(k, 2) * 8 + z_hi * 2 + lax.div(k, 2)) * 2 + core, ba)

    x_group = Group(x, lambda k: (aa, k * 4 + y_hi), x_out, x_in, (x_send, x_recv, x_ready))
    w_group = Group(
        z_lo * 2 + y_lo, w_peer, w_out, w_in, (w_send, w_recv, w_ready), 4
    )
    y_group = Group(
        y_slot(y_hi), lambda k: (aa, x * 4 + y_slot(k)), y_out, y_in, (y_send, y_recv, y_ready)
    )
    z_group = Group(
        z_hi, lambda k: ((y_lo * 8 + k * 2 + z_lo) * 2 + core, ba), z_out, z_in, (z_send, z_recv, z_ready)
    )

    barrier = pltpu.get_barrier_semaphore()
    pl.semaphore_signal(barrier, inc=1, device_id=sibling, device_id_type=MESH)
    groups = (w_group, x_group, z_group, y_group)
    for group in groups:
        group.greet(barrier)

    load_one.wait()
    put_keys(kt_one, 0, f1[...], aa * f1.shape[0])
    load_two.wait()

    core_copy = [
        pltpu.make_async_remote_copy(
            src_ref=core_out.at[u], dst_ref=core_in.at[u],
            send_sem=core_send.at[u], recv_sem=core_recv.at[u],
            device_id=sibling, device_id_type=MESH,
        )
        for u in range(4)
    ]

    def b_queries(e, parity):
        blocks = []
        for k in range(4):
            block = (k % 2) * 8 + 2 * e + k // 2
            start = pl.multiple_of((block * 2 + parity) * PART, PART)
            blocks.append(f2[pl.ds(start, PART)])
        return jnp.concatenate(blocks, axis=0)

    def a_queries(e):
        starts = [k * CHUNK + Y_ORDER[e] * PART for k in range(4)]
        return jnp.concatenate([f1[start:start + PART] for start in starts], axis=0)

    def put(out, feat, extra):
        out[0:CH] = feat
        out[CH:MSG] = extra

    def enter():
        pl.semaphore_wait(barrier, 1 + sum(group.greeted for group in groups))
        core_copy[0].start()
        for group in groups:
            group.answer()

    def share(e):
        core_copy[e].wait_recv()
        mine, got = core_own.at[e], core_in.at[e]
        feat, extra = merge([(mine[0:CH], mine[CH:MSG]), (got[0:CH], got[CH:MSG])])
        pack(feat, extra, w_out, 4 * e)
        w_group.send(e)

    def second(first_group, second_group, e):
        first_group.wait_recv(e)
        feat, extra = merge(first_group.parts(e))
        second_group.out[e, 0:PART] = feat
        second_group.out[e, PART:PACK] = extra
        second_group.send_lower(e)

    def b_other(e, *after):
        def use(feat, extra):
            put(core_out.at[e], feat, extra)
            if e:
                core_copy[e].start()
            for step in after:
                step()

        return functools.partial(b_queries, e, 1 - core), f1, kt_one, use

    def b_own(e, *after):
        def use(feat, extra):
            put(core_own.at[e], feat, extra)
            for step in after:
                step()

        return functools.partial(b_queries, e, core), f1, kt_one, use

    def a_unit(e, *after):
        def use(feat, extra):
            pack(feat, extra, x_out, 4 * e)
            if e != 1:
                x_group.send(e)
            for step in after:
                step()

        return functools.partial(a_queries, e), f2, kt_two, use

    def late_keys():
        put_keys(kt_two, 0, f2[...], ba * f2.shape[0])

    def do(step, *args):
        return functools.partial(step, *args)

    attend(
        [
            b_other(0, enter), b_own(0, late_keys), b_other(1), b_own(1), b_other(2, do(share, 0)),
            a_unit(0), b_own(2, do(share, 1)), a_unit(1), b_other(3),
            b_own(3, x_group.send_first, do(x_group.send, 1)),
            a_unit(2, do(second, w_group, z_group, 0), do(share, 2)),
            a_unit(3, do(second, w_group, z_group, 1), do(share, 3)),
        ],
        (scores_even, scores_odd),
    )
    second(x_group, y_group, 0)
    second(x_group, y_group, 1)
    for k in range(2):
        y_group.send_higher(k)
    second(x_group, y_group, 2)
    second(x_group, y_group, 3)
    for k in range(2, 4):
        y_group.send_higher(k)
    second(w_group, z_group, 2)
    second(w_group, z_group, 3)
    for k in range(4):
        z_group.send_higher(k)
    y_group.wait_recv()
    finish(y_group.parts(), (aa * 16 + ba) * PART, warped_one, flow_one)
    for e in range(4):
        core_copy[e].wait_send()
        x_group.wait_send(e)
        w_group.wait_send(e)
    z_group.wait_recv()
    finish(z_group.parts(), (ba * 32 + aa) * PART, warped_two, flow_two)
    y_group.wait_send()
    z_group.wait_send()


def emit(w1, g1, w2, g2, warped_one, flow_one, warped_two, flow_two, done):
    pairs = ((w1, warped_one), (g1, flow_one), (w2, warped_two), (g2, flow_two))
    copies = [pltpu.make_async_copy(src, dst, done.at[i]) for i, (src, dst) in enumerate(pairs)]
    for copy in copies:
        copy.start()
    for copy in copies:
        copy.wait()


def shards(frame_one, frame_two):
    rows_one, rows_two = frame_one.shape[0], frame_two.shape[0]
    vmem = pl.BlockSpec(memory_space=pltpu.VMEM)
    hbm = pl.BlockSpec(memory_space=pltpu.HBM)
    dma = pltpu.SemaphoreType.DMA
    shapes = (
        jax.ShapeDtypeStruct((PART, CH), F32),
        jax.ShapeDtypeStruct((2, PART), F32),
        jax.ShapeDtypeStruct((PART, CH), F32),
        jax.ShapeDtypeStruct((2, PART), F32),
    )
    results = pl.pallas_call(
        kernel,
        out_shape=shapes,
        in_specs=[hbm, hbm],
        out_specs=(vmem,) * 4,
        scratch_shapes=[
            pltpu.VMEM((rows_one, CH), BF16),
            pltpu.VMEM((rows_two, CH), BF16),
            pltpu.VMEM((AUG, rows_one), BF16),
            pltpu.VMEM((AUG, rows_two), BF16),
            pltpu.VMEM((rows_two, CHUNK), F32),
            pltpu.VMEM((rows_two, CHUNK), F32),
            pltpu.VMEM((4, MSG, CHUNK), F32),
            pltpu.VMEM((4, MSG, CHUNK), F32),
            pltpu.VMEM((4, MSG, CHUNK), F32),
            pltpu.VMEM((16, PACK, CH), F32),
            pltpu.VMEM((16, PACK, CH), F32),
            pltpu.VMEM((16, PACK, CH), F32),
            pltpu.VMEM((16, PACK, CH), F32),
            pltpu.VMEM((4, PACK, CH), F32),
            pltpu.VMEM((4, PACK, CH), F32),
            pltpu.VMEM((4, PACK, CH), F32),
            pltpu.VMEM((4, PACK, CH), F32),
            dma((2,)),
            dma((4,)), dma((4,)),
            dma((16,)), dma((16,)),
            dma((16,)), dma((16,)),
            dma((4,)), dma((4,)),
            dma((4,)), dma((4,)),
            pltpu.SemaphoreType.REGULAR((4,)),
            pltpu.SemaphoreType.REGULAR((4,)),
            pltpu.SemaphoreType.REGULAR((4,)),
            pltpu.SemaphoreType.REGULAR((4,)),
        ],
        compiler_params=pltpu.CompilerParams(
            collective_id=0, has_side_effects=True, vmem_limit_bytes=54976 * 1024
        ),
        name="match",
    )(frame_one, frame_two)
    return pl.pallas_call(
        emit,
        out_shape=shapes,
        in_specs=[vmem] * 4,
        out_specs=(hbm,) * 4,
        scratch_shapes=[dma((4,))],
        compiler_params=pltpu.CompilerParams(vmem_limit_bytes=1024 * 1024),
        name="emit",
    )(*results)


def solution(mesh):
    return jax.shard_map(
        shards,
        mesh=mesh,
        in_specs=(P("aa", None), P("ba", None)),
        out_specs=(
            P(("aa", "ba"), None),
            P(None, ("aa", "ba")),
            P(("ba", "aa"), None),
            P(None, ("ba", "aa")),
        ),
        check_vma=False,
    )
```
